128 devices in a mesh: row: 16 (over y, z_lo, core), col: 8 (over x, z_hi).
Axes of the slice: x: 4, y: 4, z: 4 (z_hi: 2, z_lo: 2; z = z_hi * 2 + z_lo), core: 2. Of those that a mesh axis runs over, the one named last changes fastest.
Arguments:
- features: bfloat16 [131072, 256], P('col', 'row'), may hold values from -6 to 6
- weight: bfloat16 [256, 256], replicated, may hold values from -0.375 to 0.375
- bias: float32 [256], replicated, may hold values from -3 to 3
- block_values: bfloat16 [16, 8, 384, 128, 128], P('row', 'col'), may hold values from -0.15625 to 0.15625
- block_rows: int32 [16, 8, 384], P('row', 'col'), may hold values from 0 to 63
- block_cols: int32 [16, 8, 384], P('row', 'col'), may hold values from 0 to 127
- block_count: int32 [16, 8], P('row', 'col'), may hold values from 1 to 384, as said below
- degrees: int32 [131072], replicated, may hold values from 1 to 8
- cotangent: bfloat16 [131072, 256], P(('row', 'col')), may hold values from -6 to 6
Outputs:
- activations: bfloat16 [131072, 256], P(('row', 'col'))
- weight_grad: float32 [256, 256], replicated
- feature_grad: bfloat16 [131072, 256], P('col', 'row')
The draws below stay inside these ranges and needn't reach their ends.
Inputs may be any that keep to these rules, and one draw needn't show every extreme that they name: Only the first block_count slots of a tile are live; one tile has all 384 slots live.
All inputs are finite; a program needn't handle non-finite values.
Results may differ from the reference program's by a relative error of at most 0.0059.
Values may be sent and summed in bfloat16 or wider, within the bound.
No kernel may reach another device: no remote copies, remote signals or barrier semaphores. Data moves between devices by JAX's collectives and lax.ppermute only.
A program may use at most 192 MiB of HBM per device.

```python
import math
import jax
import jax.numpy as jnp
from jax import lax

F = 256
BLK = 128
MAXB = 384
ROW_PANELS = 16
COL_PANELS = 8
NODES = 131072
ROW_BLOCKS = 64
COL_BLOCKS = 128


def draw_block_count(key, part):
    key = jax.random.fold_in(key, 11)
    first_key, second_key, pick_key = jax.random.split(key, 3)
    shape = (ROW_PANELS, COL_PANELS)
    first = jax.random.randint(first_key, shape, 1, MAXB + 1, dtype=jnp.int32)
    second = jax.random.randint(second_key, shape, 1, MAXB + 1, dtype=jnp.int32)
    counts = jnp.maximum(first * second // MAXB, 1).reshape(-1)
    pick = jax.random.randint(pick_key, (), 0, ROW_PANELS * COL_PANELS, dtype=jnp.int32)
    positions = jnp.arange(ROW_PANELS * COL_PANELS, dtype=jnp.int32)
    counts = jnp.where(positions == pick, MAXB, counts)
    return counts.reshape(shape).astype(jnp.int32)


def place_ends(values, stream_key, least, top_value):
    place = [jax.random.randint(jax.random.fold_in(stream_key, axis), (), 0, length) for axis, length in enumerate(values.shape)]
    main_axis = values.shape.index(max(values.shape))
    next_to = place[:main_axis] + [(place[main_axis] + 1) % values.shape[main_axis]] + place[main_axis + 1:]
    return values.at[tuple(place)].set(least).at[tuple(next_to)].set(top_value)


def shard_levels(own_key, shape, shards, smallest, top_value):
    loudness, own = 1.0, jax.random.fold_in(own_key, 6)
    for axis_at, shards_of in shards:
        steps = jnp.exp(jax.random.uniform(jax.random.fold_in(own, axis_at), (shards_of,), jnp.float32, smallest / len(shards), top_value / len(shards)))
        loudness = loudness * jnp.repeat(steps, shape[axis_at] // shards_of).reshape([-1 if axis == axis_at else 1 for axis in range(len(shape))])
    return loudness


def scatter_about(key, shape, scale, reach, cuts=(), kind=jnp.bfloat16):
    array = jax.random.normal(key, shape, jnp.float32) * scale
    if len(cuts) > 0:
        array = shard_levels(key, shape, cuts, -0.22, 0.18) * array
    return jnp.clip(array, min=-reach, max=reach).astype(kind)


def setup_inputs(seed: int = 0) -> dict:
    streams_of = jax.random.split(jax.random.key(seed), 10)
    features = scatter_about(streams_of[0], (NODES, F), 1.0, 6.0, ((0, 8), (1, 16)))
    weight = scatter_about(streams_of[1], (F, F), F ** -0.5, 0.375)
    bias = scatter_about(streams_of[2], (F,), 0.5, 3.0, (), jnp.float32)
    block_values = scatter_about(streams_of[3], (ROW_PANELS, COL_PANELS, MAXB, BLK, BLK), (4 * MAXB) ** -0.5, 0.15625, ((0, 16), (1, 8)))
    block_rows = place_ends(jax.random.randint(streams_of[4], (ROW_PANELS, COL_PANELS, MAXB), 0, ROW_BLOCKS), jax.random.fold_in(streams_of[4], 1), 0, ROW_BLOCKS - 1).astype(jnp.int32)
    block_cols = place_ends(jax.random.randint(streams_of[5], (ROW_PANELS, COL_PANELS, MAXB), 0, COL_BLOCKS), jax.random.fold_in(streams_of[5], 1), 0, COL_BLOCKS - 1).astype(jnp.int32)
    block_count = draw_block_count(jax.random.fold_in(streams_of[9], 71), 0)
    degrees = place_ends(jax.random.randint(streams_of[7], (NODES,), 1, 9), jax.random.fold_in(streams_of[7], 1), 1, 8).astype(jnp.int32)
    cotangent = scatter_about(streams_of[8], (NODES, F), 1.0, 6.0, ((0, 128),))
    return dict(features=features, weight=weight, bias=bias, block_values=block_values, block_rows=block_rows, block_cols=block_cols, block_count=block_count, degrees=degrees, cotangent=cotangent)


def spread(values, targets, sources, counts, source_blocks, n_target):
    tiles = ROW_PANELS * COL_PANELS
    flat_values = values.reshape(tiles, MAXB, BLK, BLK)
    flat_targets = targets.reshape(tiles, MAXB)
    flat_sources = sources.reshape(tiles, MAXB)
    flat_counts = counts.reshape(tiles)
    width = source_blocks.shape[-1]
    slot_ids = jnp.arange(MAXB, dtype=jnp.int32)

    def step(index, total):
        block = flat_values[index].astype(jnp.float32)
        live = slot_ids < flat_counts[index]
        block = jnp.where(live[:, None, None], block, jnp.zeros_like(block))
        picked = source_blocks[flat_sources[index]].astype(jnp.float32)
        return (total, block, picked, flat_targets[index])

    def forward_step(index, total):
        total, block, picked, target = step(index, total)
        product = jnp.einsum('kij,kjf->kif', block, picked)
        return total.at[target].add(product)

    def backward_step(index, total):
        total, block, picked, target = step(index, total)
        product = jnp.einsum('kij,kif->kjf', block, picked)
        return total.at[target].add(product)
    return (forward_step, backward_step, jnp.zeros((n_target, BLK, width), jnp.float32), tiles)

def reference(features, weight, bias, block_values, block_rows, block_cols, block_count, degrees, cotangent):
    scale = 1.0 / jnp.sqrt(degrees.astype(jnp.float32))
    total_blocks = NODES // BLK
    panel_ids = jnp.arange(ROW_PANELS, dtype=jnp.int32)[:, None, None]
    column_ids = jnp.arange(COL_PANELS, dtype=jnp.int32)[None, :, None]
    global_rows = panel_ids * ROW_BLOCKS + block_rows
    global_cols = column_ids * COL_BLOCKS + block_cols
    scaled_features = (scale[:, None] * features.astype(jnp.float32)).astype(jnp.bfloat16)
    forward_step, unused_step, start, tiles = spread(block_values, global_rows, global_cols, block_count, scaled_features.reshape(total_blocks, BLK, F), total_blocks)
    summed = lax.fori_loop(0, tiles, forward_step, start)
    aggregated = (scale[:, None] * summed.reshape(NODES, F)).astype(jnp.bfloat16)
    pre = jnp.dot(aggregated, weight, preferred_element_type=jnp.float32) + bias
    sigma = jax.nn.sigmoid(pre)
    activations = (pre * sigma).astype(jnp.bfloat16)
    pre_grad = (cotangent.astype(jnp.float32) * sigma * (1.0 + pre * (1.0 - sigma))).astype(jnp.bfloat16)
    weight_grad = jnp.dot(aggregated.T, pre_grad, preferred_element_type=jnp.float32) * (1.0 / math.sqrt(NODES))
    scaled_grad = (scale[:, None] * jnp.dot(pre_grad, weight.T, preferred_element_type=jnp.float32)).astype(jnp.bfloat16)
    unused_step, backward_step, start, tiles = spread(block_values, global_cols, global_rows, block_count, scaled_grad.reshape(total_blocks, BLK, F), total_blocks)
    back = lax.fori_loop(0, tiles, backward_step, start)
    feature_grad = (scale[:, None] * back.reshape(NODES, F)).astype(jnp.bfloat16)
    return (activations, weight_grad, feature_grad)
```

```python
import functools
import math

import jax
import jax.numpy as jnp
from jax import lax
from jax.experimental import pallas as pl
from jax.experimental.pallas import tpu as pltpu
from jax.sharding import PartitionSpec as P

BF16 = jnp.bfloat16
F32 = jnp.float32
CHUNK = 16
GROUP = 8


def for_live_slots(step, count_ref, values_ref, multiply, add):
    base = step * CHUNK
    count = count_ref[0]
    here = jnp.clip(count - base, 0, CHUNK)

    def one_group(turn, carry):
        first = turn * GROUP
        products = []
        for u in range(GROUP):
            block = values_ref[first + u]
            block = jnp.where(base + first + u < count, block, jnp.zeros_like(block))
            products.append(multiply(base + first + u, block))
        for u in range(GROUP):
            add(base + first + u, products[u])
        return carry

    lax.fori_loop(0, (here + GROUP - 1) // GROUP, one_group, 0)


def forward_kernel(steps, count_ref, rows_ref, cols_ref, source_ref, values_ref, out_ref, total):
    step = pl.program_id(0)
    size = values_ref.shape[1]

    @pl.when(step == 0)
    def _():
        total[...] = jnp.zeros_like(total)

    def multiply(slot, block):
        at = pl.multiple_of(cols_ref[slot] * size, size)
        return lax.dot_general(
            block,
            source_ref[:, pl.ds(at, size)],
            (((1,), (1,)), ((), ())),
            preferred_element_type=F32,
        )

    def add(slot, product):
        total[rows_ref[slot]] += product

    for_live_slots(step, count_ref, values_ref, multiply, add)

    @pl.when(step == steps - 1)
    def _():
        def write(at, carry):
            out_ref[pl.ds(pl.multiple_of(at * size, size), size), :] = total[at].astype(BF16)
            return carry

        lax.fori_loop(0, total.shape[0], write, 0)


def backward_kernel(steps, count_ref, rows_ref, cols_ref, source_ref, values_ref, out_ref, total):
    step = pl.program_id(0)
    size = values_ref.shape[1]

    @pl.when(step == 0)
    def _():
        total[...] = jnp.zeros_like(total)

    def multiply(slot, block):
        at = pl.multiple_of(rows_ref[slot] * size, size)
        return lax.dot_general(
            source_ref[pl.ds(at, size), :],
            block,
            (((0,), (0,)), ((), ())),
            preferred_element_type=F32,
        )

    def add(slot, product):
        total[cols_ref[slot]] += product

    for_live_slots(step, count_ref, values_ref, multiply, add)

    @pl.when(step == steps - 1)
    def _():
        def write(at, carry):
            out_ref[:, pl.ds(pl.multiple_of(at * size, size), size)] = total[at].astype(BF16)
            return carry

        lax.fori_loop(0, total.shape[0], write, 0)


def block_products(kernel, total_shape, out_shape, count, rows, cols, source, values):
    slots, size, _ = values.shape
    steps = slots // CHUNK

    def values_at(step, count_ref, rows_ref, cols_ref):
        last = jnp.maximum((count_ref[0] + CHUNK - 1) // CHUNK - 1, 0)
        return (jnp.minimum(step, last), 0, 0)

    return pl.pallas_call(
        functools.partial(kernel, steps),
        out_shape=jax.ShapeDtypeStruct(out_shape, BF16),
        grid_spec=pltpu.PrefetchScalarGridSpec(
            num_scalar_prefetch=3,
            grid=(steps,),
            in_specs=[
                pl.BlockSpec(memory_space=pltpu.VMEM),
                pl.BlockSpec((CHUNK, size, size), values_at),
            ],
            out_specs=pl.BlockSpec(memory_space=pltpu.VMEM),
            scratch_shapes=[pltpu.VMEM(total_shape, F32)],
        ),
        compiler_params=pltpu.CompilerParams(vmem_limit_bytes=52 * 1024 * 1024),
        cost_estimate=pl.CostEstimate(
            flops=2 * slots * size * size * source.size // 16384,
            bytes_accessed=2 * slots * size * size,
            transcendentals=0,
        ),
    )(count.reshape(1), rows, cols, source, values)


def body(
    features, weight, bias, block_values, block_rows, block_cols, block_count, degrees, cotangent
):
    row_index = lax.axis_index("row")
    col_index = lax.axis_index("col")
    n_row = lax.axis_size("row")
    n_col = lax.axis_size("col")
    values = block_values[0, 0]
    tile_rows = block_rows[0, 0]
    tile_cols = block_cols[0, 0]
    count = block_count[0, 0]
    size = values.shape[1]
    rows_dev, width = cotangent.shape
    own = features.shape[1]
    panel_rows = rows_dev * n_col
    panel_cols = rows_dev * n_row
    nodes = rows_dev * n_row * n_col
    core = row_index % 2
    chips = n_row // 2

    def scale_of(first, length):
        return 1.0 / jnp.sqrt(lax.dynamic_slice_in_dim(degrees, first, length, 0).astype(F32))

    scale_cols = scale_of(col_index * panel_cols, panel_cols)
    scale_own = scale_of(row_index * panel_rows + col_index * rows_dev, rows_dev)

    scaled = (scale_cols[None, :] * features.T.astype(F32)).astype(BF16)
    source = lax.all_gather(scaled, "row", axis=0, tiled=True)
    partial = block_products(
        forward_kernel,
        (panel_rows // size, size, width),
        (panel_rows, width),
        count,
        tile_rows,
        tile_cols,
        source,
        values,
    )
    parts = lax.all_to_all(partial.reshape(n_col, rows_dev, width), "col", 0, 0)
    reduced = jnp.sum(parts.astype(F32), axis=0)
    aggregated = (scale_own[:, None] * reduced).astype(BF16)

    pre = jnp.dot(aggregated, weight, preferred_element_type=F32) + bias
    sigma = jax.nn.sigmoid(pre)
    activations = (pre * sigma).astype(BF16)
    pre_grad = (cotangent.astype(F32) * sigma * (1.0 + pre * (1.0 - sigma))).astype(BF16)

    by_core = weight.reshape(chips, 2, own, width).transpose(1, 0, 2, 3)
    by_core = jnp.where(core == 0, by_core, by_core[::-1]).reshape(width, width)
    scaled_grad = (
        scale_own[:, None] * jnp.dot(pre_grad, by_core.T, preferred_element_type=F32)
    ).astype(BF16)
    panel_grad = lax.all_gather(scaled_grad, "col", axis=0, tiled=True)

    weight_terms = lax.dot_general(
        aggregated, pre_grad, (((0,), (0,)), ((), ())), preferred_element_type=F32
    )
    terms = lax.all_to_all(weight_terms.reshape(n_row, own, width), "row", 0, 0)
    terms = jnp.sum(terms, axis=0)
    terms = jnp.sum(lax.all_gather(terms, "col", axis=0), axis=0) * (1.0 / math.sqrt(nodes))
    weight_grad = lax.all_gather(terms, "row", axis=0, tiled=True)

    back = block_products(
        backward_kernel,
        (panel_cols // size, width, size),
        (width, panel_cols),
        count,
        tile_rows,
        tile_cols,
        panel_grad,
        values,
    )
    half = width // 2
    swapped = lax.ppermute(back[half:], "row", [(i, i ^ 1) for i in range(n_row)])
    chip_sum = (back[:half].astype(F32) + swapped.astype(F32)).astype(BF16)
    groups = [[2 * chip + c for chip in range(chips)] for c in range(2)]
    parts = lax.all_to_all(
        chip_sum.reshape(chips, own, panel_cols), "row", 0, 0, axis_index_groups=groups
    )
    back_sum = jnp.sum(parts.astype(F32), axis=0)
    feature_grad = (scale_cols[None, :] * back_sum).astype(BF16).T
    return (activations, weight_grad, feature_grad)


def solution(mesh):
    placed = (
        P("col", "row"),
        P(),
        P(),
        P("row", "col", None, None, None),
        P("row", "col", None),
        P("row", "col", None),
        P("row", "col"),
        P(),
        P(("row", "col"), None),
    )
    return jax.shard_map(
        body,
        mesh=mesh,
        in_specs=placed,
        out_specs=(P(("row", "col"), None), P(), P("col", "row")),
        check_vma=False,
    )
```

```python
import functools
import math

import jax
import jax.numpy as jnp
from jax import lax
from jax.experimental import pallas as pl
from jax.experimental.pallas import tpu as pltpu
from jax.sharding import PartitionSpec as P

BF16 = jnp.bfloat16
F32 = jnp.float32
CHUNK = 32
GROUP = 16
RING = 4
PLACES = ((1, 1), (3, 1), (2, 0), (2, 1), (1, 0), (3, 0), (0, 1), (0, 0))
ORIGINS = ((0, 0), (0, 1), (3, 0), (1, 0), (2, 0), (2, 1), (3, 1), (1, 1))


class Axis:
    def __init__(self, name, cores):
        self.name, self.cores = name, cores
        self.size = lax.axis_size(name)
        index = lax.axis_index(name)
        self.core = index % cores
        self.pair_at = index // cores % 2
        self.ring_at = index // (2 * cores)

    def index(self, ring, pair, core=0):
        at = (self.ring_at + ring) % RING * 2 + (self.pair_at + pair) % 2
        return at * self.cores + (self.core + core) % self.cores

    def ring(self, x, by):
        step = 2 * self.cores
        return lax.ppermute(x, self.name, [(i, (i + by * step) % self.size) for i in range(self.size)])

    def pair(self, x):
        return lax.ppermute(x, self.name, [(i, i ^ self.cores) for i in range(self.size)])

    def swap(self, x):
        return lax.ppermute(x, self.name, [(i, i ^ 1) for i in range(self.size)])


def add(*terms):
    return functools.reduce(jnp.add, [term.astype(F32) for term in terms])


def gather(axis, x):
    across = axis.pair(x)
    one, three = axis.ring(x, 1), axis.ring(x, 3)
    x_later, one, three = lax.optimization_barrier((x, one, three))
    two = axis.ring(x_later, 2)
    one_across, three_across = axis.pair(one), axis.pair(three)
    across, two = lax.optimization_barrier((across, two))
    two_across = axis.ring(across, 2)
    return [x, across, one, three, two, two_across, one_across, three_across]


def scatter(axis, sides, opposite, one, three, across, own, beside=None):
    n = own.shape[0]
    sides = axis.pair(sides)
    opposite = axis.ring(opposite, 2)
    sides, opposite, beside = lax.optimization_barrier((sides, opposite, beside))
    one = axis.ring(add(one, sides[:n]).astype(BF16), 1)
    three = axis.ring(add(three, sides[n:]).astype(BF16), 3)
    across = axis.pair(add(across, opposite[n:]).astype(BF16))
    return add(own, opposite[:n], one, three, across), beside


def for_live_slots(step, count_ref, values_ref, multiply, accumulate):
    base = step * CHUNK
    count = count_ref[0]
    here = jnp.clip(count - base, 0, CHUNK)

    def one_group(turn, carry):
        first = turn * GROUP
        products = []
        for u in range(GROUP):
            block = values_ref[first + u]
            block = jnp.where(base + first + u < count, block, jnp.zeros_like(block))
            products.append(multiply(base + first + u, block))
        for u in range(GROUP):
            accumulate(base + first + u, products[u])
        return carry

    lax.fori_loop(0, (here + GROUP - 1) // GROUP, one_group, 0)


def fetch(pieces, order_ref, source, sems):
    rows = pieces[0].shape[0]
    copies = []
    for i, piece in enumerate(pieces):
        at = pl.multiple_of(order_ref[i] * rows, rows)
        copies.append(pltpu.make_async_copy(piece, source.at[pl.ds(at, rows), :], sems.at[i]))
    return copies


def forward_kernel(steps, n_pieces, count_ref, rows_ref, cols_ref, order_ref, dests_ref, *refs):
    pieces, refs = refs[:n_pieces], refs[n_pieces:]
    values_ref, *outs, source, total, sems = refs
    step = pl.program_id(0)
    size = values_ref.shape[1]

    @pl.when(step == 0)
    def _():
        copies = fetch(pieces, order_ref, source, sems)
        for copy in copies:
            copy.start()
        total[...] = jnp.zeros_like(total)
        for copy in copies:
            copy.wait()

    def multiply(slot, block):
        at = pl.multiple_of(cols_ref[slot] * size, size)
        return lax.dot_general(
            block,
            source[:, pl.ds(at, size)],
            (((1,), (1,)), ((), ())),
            preferred_element_type=F32,
        )

    def accumulate(slot, product):
        total[rows_ref[slot]] += product

    for_live_slots(step, count_ref, values_ref, multiply, accumulate)

    @pl.when(step == steps - 1)
    def _():
        place = 0
        for out in outs:
            unit = total.shape[0] // len(PLACES)
            for first in range(0, out.shape[0] // size, unit):
                at = dests_ref[place] * unit
                for q in range(unit):
                    out[(first + q) * size : (first + q + 1) * size, :] = total[at + q].astype(BF16)
                place += 1


def backward_kernel(steps, n_pieces, count_ref, rows_ref, cols_ref, order_ref, *refs):
    pieces, refs = refs[:n_pieces], refs[n_pieces:]
    values_ref, *outs, source, total, sems = refs
    step = pl.program_id(0)
    size = values_ref.shape[1]

    @pl.when(step == 0)
    def _():
        copies = fetch(pieces, order_ref, source, sems)
        for copy in copies:
            copy.start()
        total[...] = jnp.zeros_like(total)
        for copy in copies:
            copy.wait()

    def multiply(slot, block):
        at = pl.multiple_of(rows_ref[slot] * size, size)
        return lax.dot_general(
            source[pl.ds(at, size), :],
            block,
            (((0,), (0,)), ((), ())),
            preferred_element_type=F32,
        )

    def accumulate(slot, product):
        total[cols_ref[slot]] += product

    for_live_slots(step, count_ref, values_ref, multiply, accumulate)

    @pl.when(step == steps - 1)
    def _():
        def write(at, carry):
            columns = pl.ds(pl.multiple_of(at * size, size), size)
            first = 0
            for out in outs:
                out[:, columns] = total[at, first : first + out.shape[0], :].astype(BF16)
                first += out.shape[0]
            return carry

        lax.fori_loop(0, total.shape[0], write, 0)


def block_products(kernel, source_shape, total_shape, out_shapes, scalars, pieces, values):
    slots, size, _ = values.shape
    steps = slots // CHUNK

    def values_at(step, count_ref, *_):
        last = jnp.maximum((count_ref[0] + CHUNK - 1) // CHUNK - 1, 0)
        return (jnp.minimum(step, last), 0, 0)

    return pl.pallas_call(
        functools.partial(kernel, steps, len(pieces)),
        out_shape=[jax.ShapeDtypeStruct(shape, BF16) for shape in out_shapes],
        grid_spec=pltpu.PrefetchScalarGridSpec(
            num_scalar_prefetch=len(scalars),
            grid=(steps,),
            in_specs=[pl.BlockSpec(memory_space=pl.ANY)] * len(pieces)
            + [pl.BlockSpec((CHUNK, size, size), values_at)],
            out_specs=[pl.BlockSpec(memory_space=pltpu.VMEM)] * len(out_shapes),
            scratch_shapes=[
                pltpu.VMEM(source_shape, BF16),
                pltpu.VMEM(total_shape, F32),
                pltpu.SemaphoreType.DMA((len(pieces),)),
            ],
        ),
        compiler_params=pltpu.CompilerParams(vmem_limit_bytes=52 * 1024 * 1024),
        cost_estimate=pl.CostEstimate(
            flops=4 * slots * size * size * 256,
            bytes_accessed=2 * slots * size * size,
            transcendentals=0,
        ),
    )(*scalars, *pieces, values)


def body(
    features, weight, bias, block_values, block_rows, block_cols, block_count, degrees, cotangent
):
    row, col = Axis("row", 2), Axis("col", 1)
    row_index, col_index = lax.axis_index("row"), lax.axis_index("col")
    values = block_values[0, 0]
    size = values.shape[1]
    rows_dev, width = cotangent.shape
    own = features.shape[1]
    panel_rows = rows_dev * col.size
    panel_cols = rows_dev * row.size
    nodes = rows_dev * row.size * col.size
    slots = (block_count[0, 0].reshape(1), block_rows[0, 0], block_cols[0, 0])

    def scale_of(first, length):
        return 1.0 / jnp.sqrt(lax.dynamic_slice_in_dim(degrees, first, length, 0).astype(F32))

    scale_cols = scale_of(col_index * panel_cols, panel_cols)
    scale_own = scale_of(row_index * panel_rows + col_index * rows_dev, rows_dev)

    def picker(owners):
        picked = (jnp.stack(owners)[:, None] * own + jnp.arange(own)[None, :]).reshape(-1)
        return (picked[:, None] == jnp.arange(width)[None, :]).astype(BF16)

    scaled = (scale_cols[None, :] * features.T.astype(F32)).astype(BF16)
    pieces = gather(row, scaled)
    pieces = pieces + [row.swap(piece) for piece in pieces]
    order = jnp.stack([row.index(r, p, c) for c in (0, 1) for r, p in ORIGINS])
    dests = jnp.stack([col.index(r, p) for r, p in PLACES])
    partial = block_products(
        forward_kernel,
        (width, panel_cols),
        (panel_rows // size, size, width),
        [(2 * rows_dev, width)] * 2 + [(rows_dev, width)] * 4,
        slots + (order, dests),
        pieces,
        values,
    )
    reduced, _ = scatter(col, *partial)
    aggregated = (scale_own[:, None] * reduced).astype(BF16)

    pre = jnp.dot(aggregated, weight, preferred_element_type=F32) + bias
    sigma = jax.nn.sigmoid(pre)
    activations = (pre * sigma).astype(BF16)
    pre_grad = (cotangent.astype(F32) * sigma * (1.0 + pre * (1.0 - sigma))).astype(BF16)

    to_places = picker([row.index(r, p, c) for c in (1, 0) for r, p in PLACES])
    weight_places = jnp.dot(to_places, weight, preferred_element_type=F32).astype(BF16)
    scaled_grad = (
        scale_own[:, None] * jnp.dot(pre_grad, weight_places.T, preferred_element_type=F32)
    ).astype(BF16)
    pieces = gather(col, scaled_grad)

    near = [(r, p, c) for c in (0, 1) for p in (0, 1) for r in range(RING)]
    to_near = picker([row.index(*place) for place in near])
    agg_near = lax.dot_general(
        aggregated, to_near, (((1,), (1,)), ((), ())), preferred_element_type=F32
    ).astype(BF16)
    terms = lax.dot_general(
        agg_near, pre_grad, (((0,), (0,)), ((), ())), preferred_element_type=F32
    )
    terms = terms[: width // 2] + row.swap(terms[width // 2 :])
    terms = terms[: width // 4] + row.pair(terms[width // 4 :])
    terms = sum(
        [row.ring(terms[by * own : (by + 1) * own], by) for by in range(1, RING)], terms[:own]
    )
    terms = terms + col.pair(terms)
    terms = (terms + col.ring(terms, 2)) + (col.ring(terms, 1) + col.ring(terms, 3))
    terms = terms * (1.0 / math.sqrt(nodes))
    pieces, terms = lax.optimization_barrier((pieces, terms))
    terms = jnp.concatenate([terms] + [row.ring(terms, by) for by in range(1, RING)], axis=0)
    terms = jnp.concatenate([terms, row.pair(terms)], axis=0)
    terms = jnp.concatenate([terms, row.swap(terms)], axis=0)
    order = jnp.stack([col.index(r, p) for r, p in ORIGINS])
    other, *mine = block_products(
        backward_kernel,
        (panel_rows, width),
        (panel_cols // size, width, size),
        [(8 * own, panel_cols)] + [(2 * own, panel_cols)] * 2 + [(own, panel_cols)] * 4,
        slots + (order,),
        pieces,
        values,
    )
    other = row.swap(other)
    first, chip_sums = 0, []
    for part in mine:
        last = first + part.shape[0]
        chip_sums.append(add(part, other[first:last]).astype(BF16))
        first = last
    reduced, terms = scatter(row, *chip_sums, beside=terms)
    feature_grad = (scale_cols[None, :] * reduced).astype(BF16).T
    place_of = {
        (-by % RING, p, c): (c * 2 + p) * RING + by
        for c in (0, 1)
        for p in (0, 1)
        for by in range(RING)
    }
    held = jnp.zeros((row.size,), jnp.int32)
    for offsets, at in place_of.items():
        held = jnp.where(jnp.arange(row.size) == row.index(*offsets), at, held)
    weight_grad = jnp.take(terms.reshape(row.size, own, width), held, axis=0).reshape(width, width)
    return (activations, weight_grad, feature_grad)


def solution(mesh):
    placed = (
        P("col", "row"),
        P(),
        P(),
        P("row", "col", None, None, None),
        P("row", "col", None),
        P("row", "col", None),
        P("row", "col"),
        P(),
        P(("row", "col"), None),
    )
    return jax.shard_map(
        body,
        mesh=mesh,
        in_specs=placed,
        out_specs=(P(("row", "col"), None), P(), P("col", "row")),
        check_vma=False,
    )
```

```python
import functools
import math

import jax
import jax.numpy as jnp
from jax import lax
from jax.experimental import pallas as pl
from jax.experimental.pallas import tpu as pltpu
from jax.sharding import PartitionSpec as P

BF16 = jnp.bfloat16
F32 = jnp.float32
CHUNK = 64
GROUP = 64
RING = 4
PLACES = ((1, 1), (3, 1), (2, 0), (2, 1), (1, 0), (3, 0), (0, 1), (0, 0))
ORIGINS = ((0, 0), (0, 1), (3, 0), (1, 0), (2, 0), (2, 1), (3, 1), (1, 1))


class Axis:
    def __init__(self, name, cores):
        self.name, self.cores = name, cores
        self.size = lax.axis_size(name)
        index = lax.axis_index(name)
        self.core = index % cores
        self.pair_at = index // cores % 2
        self.ring_at = index // (2 * cores)

    def index(self, ring, pair, core=0):
        at = (self.ring_at + ring) % RING * 2 + (self.pair_at + pair) % 2
        return at * self.cores + (self.core + core) % self.cores

    def ring(self, x, by):
        step = 2 * self.cores
        return lax.ppermute(x, self.name, [(i, (i + by * step) % self.size) for i in range(self.size)])

    def pair(self, x):
        return lax.ppermute(x, self.name, [(i, i ^ self.cores) for i in range(self.size)])

    def swap(self, x):
        return lax.ppermute(x, self.name, [(i, i ^ 1) for i in range(self.size)])


def both_pairs(row, col, x):
    n = col.size
    to = [
        (r * n + c, (r ^ row.cores) * n + (c ^ col.cores))
        for r in range(row.size)
        for c in range(n)
    ]
    return lax.ppermute(x, (row.name, col.name), to)


def add(*terms):
    return functools.reduce(jnp.add, [term.astype(F32) for term in terms])


def gather(axis, x):
    across = axis.pair(x)
    one, three = axis.ring(x, 1), axis.ring(x, 3)
    x_later, across, one, three = lax.optimization_barrier((x, across, one, three))
    one_across, three_across = axis.pair(one), axis.pair(three)
    two, two_across = axis.ring(x_later, 2), axis.ring(across, 2)
    return [x, across, one, three, two, two_across, one_across, three_across]


def scatter(axis, sides, opposite, one, three, across, own, beside=None):
    n = own.shape[0]
    sides = axis.pair(sides)
    opposite = axis.ring(opposite, 2)
    sides, opposite, beside = lax.optimization_barrier((sides, opposite, beside))
    one = axis.ring(add(one, sides[:n]).astype(BF16), 1)
    three = axis.ring(add(three, sides[n:]).astype(BF16), 3)
    across = axis.pair(add(across, opposite[n:]).astype(BF16))
    return add(own, opposite[:n], one, three, across), beside


def for_live_slots(step, count_ref, values_ref, multiply, accumulate):
    base = step * CHUNK
    count = count_ref[0, 0]
    here = jnp.clip(count - base, 0, CHUNK)

    def one_group(turn, carry):
        first = turn * GROUP
        products = []
        for u in range(GROUP):
            block = values_ref[first + u]
            block = jnp.where(base + first + u < count, block, jnp.zeros_like(block))
            products.append(multiply(base + first + u, block))
        for u in range(GROUP):
            accumulate(base + first + u, products[u])
        return carry

    lax.fori_loop(0, (here + GROUP - 1) // GROUP, one_group, 0)


def fetch(pieces, order_ref, source, sems):
    rows = pieces[0].shape[0]
    copies = []
    for i, piece in enumerate(pieces):
        at = pl.multiple_of(order_ref[i] * rows, rows)
        copies.append(pltpu.make_async_copy(piece, source.at[pl.ds(at, rows), :], sems.at[i]))
    return copies


def forward_kernel(steps, n_pieces, count_ref, rows_ref, cols_ref, order_ref, dests_ref, *refs):
    pieces, refs = refs[:n_pieces], refs[n_pieces:]
    values_ref, *outs, source, total, sems = refs
    step = pl.program_id(0)
    size = values_ref.shape[1]

    @pl.when(step == 0)
    def _():
        copies = fetch(pieces, order_ref, source, sems)
        for copy in copies:
            copy.start()
        total[...] = jnp.zeros_like(total)
        for copy in copies:
            copy.wait()

    def multiply(slot, block):
        at = pl.multiple_of(cols_ref[0, slot] * size, size)
        return lax.dot_general(
            block,
            source[:, pl.ds(at, size)],
            (((1,), (1,)), ((), ())),
            preferred_element_type=F32,
        )

    def accumulate(slot, product):
        total[rows_ref[0, slot]] += product

    for_live_slots(step, count_ref, values_ref, multiply, accumulate)

    @pl.when(step == steps - 1)
    def _():
        place = 0
        for out in outs:
            unit = total.shape[0] // len(PLACES)
            for first in range(0, out.shape[0] // size, unit):
                at = dests_ref[place] * unit
                for q in range(unit):
                    out[(first + q) * size : (first + q + 1) * size, :] = total[at + q].astype(BF16)
                place += 1


def backward_kernel(steps, n_pieces, count_ref, rows_ref, cols_ref, order_ref, *refs):
    pieces, refs = refs[:n_pieces], refs[n_pieces:]
    values_ref, *outs, source, total, sems = refs
    step = pl.program_id(0)
    size = values_ref.shape[1]

    @pl.when(step == 0)
    def _():
        copies = fetch(pieces, order_ref, source, sems)
        for copy in copies:
            copy.start()
        total[...] = jnp.zeros_like(total)
        for copy in copies:
            copy.wait()

    def multiply(slot, block):
        at = pl.multiple_of(rows_ref[0, slot] * size, size)
        return lax.dot_general(
            source[pl.ds(at, size), :],
            block,
            (((0,), (0,)), ((), ())),
            preferred_element_type=F32,
        )

    def accumulate(slot, product):
        total[cols_ref[0, slot]] += product

    for_live_slots(step, count_ref, values_ref, multiply, accumulate)

    @pl.when(step == steps - 1)
    def _():
        def write(at, carry):
            columns = pl.ds(pl.multiple_of(at * size, size), size)
            first = 0
            for out in outs:
                out[:, columns] = total[at, first : first + out.shape[0], :].astype(BF16)
                first += out.shape[0]
            return carry

        lax.fori_loop(0, total.shape[0], write, 0)


def block_products(kernel, source_shape, total_shape, out_shapes, scalars, pieces, values):
    slots, size, _ = values.shape
    steps = slots // CHUNK

    def values_at(step, count_ref, *_):
        last = jnp.maximum((count_ref[0, 0] + CHUNK - 1) // CHUNK - 1, 0)
        return (jnp.minimum(step, last), 0, 0)

    return pl.pallas_call(
        functools.partial(kernel, steps, len(pieces)),
        out_shape=[jax.ShapeDtypeStruct(shape, BF16) for shape in out_shapes],
        grid_spec=pltpu.PrefetchScalarGridSpec(
            num_scalar_prefetch=len(scalars),
            grid=(steps,),
            in_specs=[pl.BlockSpec(memory_space=pl.ANY)] * len(pieces)
            + [pl.BlockSpec((CHUNK, size, size), values_at)],
            out_specs=[pl.BlockSpec(memory_space=pltpu.VMEM)] * len(out_shapes),
            scratch_shapes=[
                pltpu.VMEM(source_shape, BF16),
                pltpu.VMEM(total_shape, F32),
                pltpu.SemaphoreType.DMA((len(pieces),)),
            ],
        ),
        compiler_params=pltpu.CompilerParams(vmem_limit_bytes=52 * 1024 * 1024),
        cost_estimate=pl.CostEstimate(
            flops=4 * slots * size * size * 256,
            bytes_accessed=2 * slots * size * size,
            transcendentals=0,
        ),
    )(*scalars, *pieces, values)


def body(
    features, weight, bias, block_values, block_rows, block_cols, block_count, degrees, cotangent
):
    row, col = Axis("row", 2), Axis("col", 1)
    row_index, col_index = lax.axis_index("row"), lax.axis_index("col")
    values = block_values[0, 0]
    size = values.shape[1]
    rows_dev, width = cotangent.shape
    own = features.shape[1]
    panel_rows = rows_dev * col.size
    panel_cols = rows_dev * row.size
    nodes = rows_dev * row.size * col.size
    slots = (block_count, block_rows[0], block_cols[0])

    def scale_of(first, length):
        return 1.0 / jnp.sqrt(lax.dynamic_slice_in_dim(degrees, first, length, 0).astype(F32))

    scale_cols = scale_of(col_index * panel_cols, panel_cols)
    scale_own = scale_of(row_index * panel_rows + col_index * rows_dev, rows_dev)

    def picker(owners):
        picked = (jnp.stack(owners)[:, None] * own + jnp.arange(own)[None, :]).reshape(-1)
        return (picked[:, None] == jnp.arange(width)[None, :]).astype(BF16)

    scaled = (scale_cols[None, :] * features.T.astype(F32)).astype(BF16)
    pieces = gather(row, scaled)
    pieces = pieces + [row.swap(piece) for piece in pieces]
    order = jnp.stack([row.index(r, p, c) for c in (0, 1) for r, p in ORIGINS])
    dests = jnp.stack([col.index(r, p) for r, p in PLACES])
    partial = block_products(
        forward_kernel,
        (width, panel_cols),
        (panel_rows // size, size, width),
        [(2 * rows_dev, width)] * 2 + [(rows_dev, width)] * 4,
        slots + (order, dests),
        pieces,
        values,
    )
    reduced, _ = scatter(col, *partial)
    aggregated = (scale_own[:, None] * reduced).astype(BF16)

    pre = jnp.dot(aggregated, weight, preferred_element_type=F32) + bias
    sigma = jax.nn.sigmoid(pre)
    activations = (pre * sigma).astype(BF16)
    pre_grad = (cotangent.astype(F32) * sigma * (1.0 + pre * (1.0 - sigma))).astype(BF16)

    to_places = picker([row.index(r, p, c) for c in (1, 0) for r, p in PLACES])
    weight_places = jnp.dot(to_places, weight, preferred_element_type=F32).astype(BF16)
    scaled_grad = (
        scale_own[:, None] * jnp.dot(pre_grad, weight_places.T, preferred_element_type=F32)
    ).astype(BF16)
    pieces = gather(col, scaled_grad)

    near = [(r, p - row.pair_at, c) for c in (0, 1) for r in range(RING) for p in (0, 1)]
    to_near = picker([row.index(*place) for place in near])
    agg_near = lax.dot_general(
        aggregated, to_near, (((1,), (1,)), ((), ())), preferred_element_type=F32
    ).astype(BF16)
    terms = lax.dot_general(
        agg_near, pre_grad, (((0,), (0,)), ((), ())), preferred_element_type=F32
    )
    terms = terms[: width // 2] + row.swap(terms[width // 2 :])
    part = terms.shape[0] // RING
    terms = sum(
        [row.ring(terms[by * part : (by + 1) * part], by) for by in range(1, RING)], terms[:part]
    )
    pieces, terms = lax.optimization_barrier((pieces, terms))
    pairs = [terms, row.pair(terms), col.pair(terms), both_pairs(row, col, terms)]

    order = jnp.stack([col.index(r, p) for r, p in ORIGINS])
    first_half, second_half, *mine = block_products(
        backward_kernel,
        (panel_rows, width),
        (panel_cols // size, width, size),
        [(4 * own, panel_cols)] * 2 + [(2 * own, panel_cols)] * 2 + [(own, panel_cols)] * 4,
        slots + (order,),
        pieces,
        values,
    )
    first_half, second_half, pairs = lax.optimization_barrier((first_half, second_half, pairs))
    first_half = row.swap(first_half)
    terms = (pairs[0] + pairs[1]) + (pairs[2] + pairs[3])
    terms = (terms + col.ring(terms, 2)) + (col.ring(terms, 1) + col.ring(terms, 3))
    terms = terms * (1.0 / math.sqrt(nodes))
    second_half = row.swap(second_half)
    first_half, terms = lax.optimization_barrier((first_half, terms))
    around = [terms] + [row.ring(terms, by) for by in range(1, RING)]
    sides = add(mine[0], first_half[: 2 * own]).astype(BF16)
    opposite = add(mine[1], first_half[2 * own :]).astype(BF16)
    second_half, sides, opposite = lax.optimization_barrier((second_half, sides, opposite))
    rest = [
        add(part, second_half[i * own : (i + 1) * own]).astype(BF16)
        for i, part in enumerate(mine[2:])
    ]
    reduced, around = scatter(row, sides, opposite, *rest, beside=around)
    feature_grad = (scale_cols[None, :] * reduced).astype(BF16).T
    terms = jnp.concatenate(around, axis=0)
    terms = jnp.concatenate([terms, row.swap(terms)], axis=0)
    held = jnp.zeros((row.size,), jnp.int32)
    for c in (0, 1):
        for by in range(RING):
            for p in (0, 1):
                owner = row.index(-by, p - row.pair_at, c)
                held = jnp.where(jnp.arange(row.size) == owner, (c * RING + by) * 2 + p, held)
    weight_grad = jnp.take(terms.reshape(row.size, own, width), held, axis=0).reshape(width, width)
    return (activations, weight_grad, feature_grad)


def solution(mesh):
    placed = (
        P("col", "row"),
        P(),
        P(),
        P("row", "col", None, None, None),
        P("row", "col", None),
        P("row", "col", None),
        P("row", "col"),
        P(),
        P(("row", "col"), None),
    )
    return jax.shard_map(
        body,
        mesh=mesh,
        in_specs=placed,
        out_specs=(P(("row", "col"), None), P(), P("col", "row")),
        check_vma=False,
    )
```

```python
import functools
import math

import jax
import jax.numpy as jnp
from jax import lax
from jax.experimental import pallas as pl
from jax.experimental.pallas import tpu as pltpu
from jax.sharding import PartitionSpec as P

BF16 = jnp.bfloat16
F32 = jnp.float32
CHUNK = 64
GROUP = 64
RING = 4
PLACES = ((1, 1), (3, 1), (2, 0), (2, 1), (1, 0), (3, 0), (0, 1), (0, 0))
ORIGINS = ((0, 0), (0, 1), (3, 0), (1, 0), (2, 0), (2, 1), (3, 1), (1, 1))


class Axis:
    def __init__(self, name, cores):
        self.name, self.cores = name, cores
        self.size = lax.axis_size(name)
        index = lax.axis_index(name)
        self.core = index % cores
        self.pair_at = index // cores % 2
        self.ring_at = index // (2 * cores)

    def index(self, ring, pair, core=0):
        at = (self.ring_at + ring) % RING * 2 + (self.pair_at + pair) % 2
        return at * self.cores + (self.core + core) % self.cores

    def ring(self, x, by):
        step = 2 * self.cores
        return lax.ppermute(x, self.name, [(i, (i + by * step) % self.size) for i in range(self.size)])

    def pair(self, x):
        return lax.ppermute(x, self.name, [(i, i ^ self.cores) for i in range(self.size)])

    def swap(self, x):
        return lax.ppermute(x, self.name, [(i, i ^ 1) for i in range(self.size)])


def both_pairs(row, col, x):
    n = col.size
    to = [
        (r * n + c, (r ^ row.cores) * n + (c ^ col.cores))
        for r in range(row.size)
        for c in range(n)
    ]
    return lax.ppermute(x, (row.name, col.name), to)


def add(*terms):
    return functools.reduce(jnp.add, [term.astype(F32) for term in terms])


def gather_first(axis, x):
    return list(
        lax.optimization_barrier((x, axis.pair(x), axis.ring(x, 1), axis.ring(x, 3)))
    )


def gather_second(axis, first):
    x, across, one, three = first
    return [axis.ring(x, 2), axis.ring(across, 2), axis.pair(one), axis.pair(three)]


def scatter_first(axis, sides, opposite):
    return axis.pair(sides), axis.ring(opposite, 2)


def scatter_second(axis, sides, opposite, one, three, across, own):
    n = own.shape[0]
    one = axis.ring(add(one, sides[:n]).astype(BF16), 1)
    three = axis.ring(add(three, sides[n:]).astype(BF16), 3)
    across = axis.pair(add(across, opposite[n:]).astype(BF16))
    return add(own, opposite[:n], one, three, across)


def for_live_slots(step, count_ref, values_ref, multiply, accumulate):
    base = step * CHUNK
    count = count_ref[0, 0]
    here = jnp.clip(count - base, 0, CHUNK)

    def one_group(turn, carry):
        first = turn * GROUP
        products = []
        for u in range(GROUP):
            block = values_ref[first + u]
            block = jnp.where(base + first + u < count, block, jnp.zeros_like(block))
            products.append(multiply(base + first + u, block))
        for u in range(GROUP):
            accumulate(base + first + u, products[u])
        return carry

    lax.fori_loop(0, (here + GROUP - 1) // GROUP, one_group, 0)


def fetch(pieces, order_ref, source, sems):
    rows = pieces[0].shape[0]
    copies = []
    for i, piece in enumerate(pieces):
        at = pl.multiple_of(order_ref[i] * rows, rows)
        copies.append(pltpu.make_async_copy(piece, source.at[pl.ds(at, rows), :], sems.at[i]))
    return copies


def forward_kernel(steps, n_pieces, count_ref, rows_ref, cols_ref, order_ref, dests_ref, *refs):
    pieces, refs = refs[:n_pieces], refs[n_pieces:]
    values_ref, *outs, source, total, sems = refs
    step = pl.program_id(0)
    size = values_ref.shape[1]

    @pl.when(step == 0)
    def _():
        copies = fetch(pieces, order_ref, source, sems)
        for copy in copies:
            copy.start()
        total[...] = jnp.zeros_like(total)
        for copy in copies:
            copy.wait()

    def multiply(slot, block):
        at = pl.multiple_of(cols_ref[0, slot] * size, size)
        return lax.dot_general(
            block,
            source[:, pl.ds(at, size)],
            (((1,), (1,)), ((), ())),
            preferred_element_type=F32,
        )

    def accumulate(slot, product):
        total[rows_ref[0, slot]] += product

    for_live_slots(step, count_ref, values_ref, multiply, accumulate)

    @pl.when(step == steps - 1)
    def _():
        place = 0
        for out in outs:
            unit = total.shape[0] // len(PLACES)
            for first in range(0, out.shape[0] // size, unit):
                at = dests_ref[place] * unit
                for q in range(unit):
                    out[(first + q) * size : (first + q + 1) * size, :] = total[at + q].astype(BF16)
                place += 1


def backward_kernel(steps, n_pieces, count_ref, rows_ref, cols_ref, order_ref, *refs):
    pieces, refs = refs[:n_pieces], refs[n_pieces:]
    values_ref, *outs, source, total, sems = refs
    step = pl.program_id(0)
    size = values_ref.shape[1]

    @pl.when(step == 0)
    def _():
        copies = fetch(pieces, order_ref, source, sems)
        for copy in copies:
            copy.start()
        total[...] = jnp.zeros_like(total)
        for copy in copies:
            copy.wait()

    def multiply(slot, block):
        at = pl.multiple_of(rows_ref[0, slot] * size, size)
        return lax.dot_general(
            source[pl.ds(at, size), :],
            block,
            (((0,), (0,)), ((), ())),
            preferred_element_type=F32,
        )

    def accumulate(slot, product):
        total[cols_ref[0, slot]] += product

    for_live_slots(step, count_ref, values_ref, multiply, accumulate)

    @pl.when(step == steps - 1)
    def _():
        def write(at, carry):
            columns = pl.ds(pl.multiple_of(at * size, size), size)
            first = 0
            for out in outs:
                out[:, columns] = total[at, first : first + out.shape[0], :].astype(BF16)
                first += out.shape[0]
            return carry

        lax.fori_loop(0, total.shape[0], write, 0)


def block_products(kernel, source_shape, total_shape, out_shapes, scalars, pieces, values):
    slots, size, _ = values.shape
    steps = slots // CHUNK

    def values_at(step, count_ref, *_):
        last = jnp.maximum((count_ref[0, 0] + CHUNK - 1) // CHUNK - 1, 0)
        return (jnp.minimum(step, last), 0, 0)

    return pl.pallas_call(
        functools.partial(kernel, steps, len(pieces)),
        out_shape=[jax.ShapeDtypeStruct(shape, BF16) for shape in out_shapes],
        grid_spec=pltpu.PrefetchScalarGridSpec(
            num_scalar_prefetch=len(scalars),
            grid=(steps,),
            in_specs=[pl.BlockSpec(memory_space=pl.ANY)] * len(pieces)
            + [pl.BlockSpec((CHUNK, size, size), values_at)],
            out_specs=[pl.BlockSpec(memory_space=pltpu.VMEM)] * len(out_shapes),
            scratch_shapes=[
                pltpu.VMEM(source_shape, BF16),
                pltpu.VMEM(total_shape, F32),
                pltpu.SemaphoreType.DMA((len(pieces),)),
            ],
        ),
        compiler_params=pltpu.CompilerParams(vmem_limit_bytes=52 * 1024 * 1024),
        cost_estimate=pl.CostEstimate(
            flops=4 * slots * size * size * 256,
            bytes_accessed=2 * slots * size * size,
            transcendentals=0,
        ),
    )(*scalars, *pieces, values)


def body(
    features, weight, bias, block_values, block_rows, block_cols, block_count, degrees, cotangent
):
    row, col = Axis("row", 2), Axis("col", 1)
    row_index, col_index = lax.axis_index("row"), lax.axis_index("col")
    values = block_values[0, 0]
    size = values.shape[1]
    rows_dev, width = cotangent.shape
    own = features.shape[1]
    panel_rows = rows_dev * col.size
    panel_cols = rows_dev * row.size
    nodes = rows_dev * row.size * col.size
    slots = (block_count, block_rows[0], block_cols[0])

    def scale_of(first, length):
        return 1.0 / jnp.sqrt(lax.dynamic_slice_in_dim(degrees, first, length, 0).astype(F32))

    scale_cols = scale_of(col_index * panel_cols, panel_cols)
    scale_own = scale_of(row_index * panel_rows + col_index * rows_dev, rows_dev)

    def picker(owners):
        picked = (jnp.stack(owners)[:, None] * own + jnp.arange(own)[None, :]).reshape(-1)
        return (picked[:, None] == jnp.arange(width)[None, :]).astype(BF16)

    scaled = (scale_cols[None, :] * features.T.astype(F32)).astype(BF16)
    dests = jnp.stack([col.index(r, p) for r, p in PLACES])

    def half_products(pieces):
        pieces = pieces + [row.swap(piece) for piece in pieces]
        return block_products(
            forward_kernel,
            (width // 2, panel_cols),
            (panel_rows // size, size, width // 2),
            [(2 * rows_dev, width // 2)] * 2 + [(rows_dev, width // 2)] * 4,
            slots + (jnp.arange(len(pieces), dtype=jnp.int32), dests),
            pieces,
            values,
        )

    near_pieces = gather_first(row, scaled)
    far_pieces = gather_second(row, near_pieces)
    partial = half_products(near_pieces)
    partial, far_pieces = lax.optimization_barrier((partial, far_pieces))
    arrived = scatter_first(col, *partial[:2])
    far_partial = half_products(far_pieces)
    far_partial, arrived = lax.optimization_barrier((far_partial, arrived))
    far_arrived = scatter_first(col, *far_partial[:2])
    reduced = scatter_second(col, *arrived, *partial[2:])
    far_reduced = scatter_second(col, *far_arrived, *far_partial[2:])
    reduced = jnp.concatenate([reduced, far_reduced], axis=1)
    aggregated = (scale_own[:, None] * reduced).astype(BF16)

    to_held = picker(
        [row.index(r, p, c) for half in (ORIGINS[:4], ORIGINS[4:]) for c in (0, 1) for r, p in half]
    )
    weight_held = jnp.dot(to_held, weight, preferred_element_type=F32).astype(BF16)
    pre = jnp.dot(aggregated, weight_held, preferred_element_type=F32) + bias
    sigma = jax.nn.sigmoid(pre)
    activations = (pre * sigma).astype(BF16)
    pre_grad = (cotangent.astype(F32) * sigma * (1.0 + pre * (1.0 - sigma))).astype(BF16)

    to_places = picker([row.index(r, p, c) for c in (1, 0) for r, p in PLACES])
    weight_places = jnp.dot(to_places, weight, preferred_element_type=F32).astype(BF16)
    scaled_grad = (
        scale_own[:, None] * jnp.dot(pre_grad, weight_places.T, preferred_element_type=F32)
    ).astype(BF16)
    pieces = gather_first(col, scaled_grad)
    pieces = pieces + gather_second(col, pieces)

    near = [(r, p - row.pair_at, c) for c in (0, 1) for r in range(RING) for p in (0, 1)]
    to_near = picker([row.index(*place) for place in near])
    to_near = jnp.dot(to_near, to_held.T, preferred_element_type=F32).astype(BF16)
    agg_near = lax.dot_general(
        aggregated, to_near, (((1,), (1,)), ((), ())), preferred_element_type=F32
    ).astype(BF16)
    terms = lax.dot_general(
        agg_near, pre_grad, (((0,), (0,)), ((), ())), preferred_element_type=F32
    )
    terms = terms[: width // 2] + row.swap(terms[width // 2 :])
    part = terms.shape[0] // RING
    terms = sum(
        [row.ring(terms[by * part : (by + 1) * part], by) for by in range(1, RING)], terms[:part]
    )
    pieces, terms = lax.optimization_barrier((pieces, terms))
    pairs = [terms, row.pair(terms), col.pair(terms), both_pairs(row, col, terms)]

    order = jnp.stack([col.index(r, p) for r, p in ORIGINS])
    first_half, second_half, *mine = block_products(
        backward_kernel,
        (panel_rows, width),
        (panel_cols // size, width, size),
        [(4 * own, panel_cols)] * 2 + [(2 * own, panel_cols)] * 2 + [(own, panel_cols)] * 4,
        slots + (order,),
        pieces,
        values,
    )
    first_half, second_half, pairs = lax.optimization_barrier((first_half, second_half, pairs))
    first_half = row.swap(first_half)
    terms = (pairs[0] + pairs[1]) + (pairs[2] + pairs[3])
    terms = (terms + col.ring(terms, 2)) + (col.ring(terms, 1) + col.ring(terms, 3))
    terms = terms * (1.0 / math.sqrt(nodes))
    second_half = row.swap(second_half)
    first_half, terms = lax.optimization_barrier((first_half, terms))
    around = [terms] + [row.ring(terms, by) for by in range(1, RING)]
    sides = add(mine[0], first_half[: 2 * own]).astype(BF16)
    opposite = add(mine[1], first_half[2 * own :]).astype(BF16)
    second_half, sides, opposite = lax.optimization_barrier((second_half, sides, opposite))
    rest = [
        add(part, second_half[i * own : (i + 1) * own]).astype(BF16)
        for i, part in enumerate(mine[2:])
    ]
    arrived = scatter_first(row, sides, opposite)
    arrived, around = lax.optimization_barrier((arrived, around))
    reduced = scatter_second(row, *arrived, *rest)
    feature_grad = (scale_cols[None, :] * reduced).astype(BF16).T
    terms = jnp.concatenate(around, axis=0)
    terms = jnp.concatenate([terms, row.swap(terms)], axis=0)
    held = jnp.zeros((row.size,), jnp.int32)
    for c in (0, 1):
        for by in range(RING):
            for p in (0, 1):
                owner = row.index(-by, p - row.pair_at, c)
                held = jnp.where(jnp.arange(row.size) == owner, (c * RING + by) * 2 + p, held)
    weight_grad = jnp.take(terms.reshape(row.size, own, width), held, axis=0).reshape(width, width)
    return (activations, weight_grad, feature_grad)


def solution(mesh):
    placed = (
        P("col", "row"),
        P(),
        P(),
        P("row", "col", None, None, None),
        P("row", "col", None),
        P("row", "col", None),
        P("row", "col"),
        P(),
        P(("row", "col"), None),
    )
    return jax.shard_map(
        body,
        mesh=mesh,
        in_specs=placed,
        out_specs=(P(("row", "col"), None), P(), P("col", "row")),
        check_vma=False,
    )
```

```python
import functools
import math

import jax
import jax.numpy as jnp
from jax import lax
from jax.experimental import pallas as pl
from jax.experimental.pallas import tpu as pltpu
from jax.sharding import PartitionSpec as P

BF16 = jnp.bfloat16
F32 = jnp.float32
CHUNK = 64
GROUP = 64
RING = 4
PLACES = ((1, 1), (3, 1), (2, 0), (2, 1), (1, 0), (3, 0), (0, 1), (0, 0))
ORIGINS = ((0, 0), (0, 1), (3, 0), (1, 0), (2, 0), (2, 1), (3, 1), (1, 1))


class Axis:
    def __init__(self, name, cores):
        self.name, self.cores = name, cores
        self.size = lax.axis_size(name)
        index = lax.axis_index(name)
        self.core = index % cores
        self.pair_at = index // cores % 2
        self.ring_at = index // (2 * cores)

    def index(self, ring, pair, core=0):
        at = (self.ring_at + ring) % RING * 2 + (self.pair_at + pair) % 2
        return at * self.cores + (self.core + core) % self.cores

    def ring(self, x, by):
        step = 2 * self.cores
        return lax.ppermute(x, self.name, [(i, (i + by * step) % self.size) for i in range(self.size)])

    def pair(self, x):
        return lax.ppermute(x, self.name, [(i, i ^ self.cores) for i in range(self.size)])

    def swap(self, x):
        return lax.ppermute(x, self.name, [(i, i ^ 1) for i in range(self.size)])


def both_pairs(row, col, x):
    n = col.size
    to = [
        (r * n + c, (r ^ row.cores) * n + (c ^ col.cores))
        for r in range(row.size)
        for c in range(n)
    ]
    return lax.ppermute(x, (row.name, col.name), to)


def add(*terms):
    return functools.reduce(jnp.add, [term.astype(F32) for term in terms])


def gather_first(axis, x):
    return list(
        lax.optimization_barrier((x, axis.pair(x), axis.ring(x, 1), axis.ring(x, 3)))
    )


def gather_second(axis, first):
    x, across, one, three = first
    return [axis.ring(x, 2), axis.ring(across, 2), axis.pair(one), axis.pair(three)]


def scatter_first(axis, sides, opposite):
    return axis.pair(sides), axis.ring(opposite, 2)


def scatter_second(axis, sides, opposite, one, three, across, own):
    n = own[0].shape[0]
    one = axis.ring(add(*one, sides[:n]).astype(BF16), 1)
    three = axis.ring(add(*three, sides[n:]).astype(BF16), 3)
    across = axis.pair(add(*across, opposite[n:]).astype(BF16))
    return add(*own, opposite[:n], one, three, across)


def for_live_slots(step, count_ref, values_ref, multiply, accumulate):
    base = step * CHUNK
    count = count_ref[0, 0]
    here = jnp.clip(count - base, 0, CHUNK)

    def one_group(turn, carry):
        first = turn * GROUP
        products = []
        for u in range(GROUP):
            block = values_ref[first + u]
            block = jnp.where(base + first + u < count, block, jnp.zeros_like(block))
            products.append(multiply(base + first + u, block))
        for u in range(GROUP):
            accumulate(base + first + u, products[u])
        return carry

    lax.fori_loop(0, (here + GROUP - 1) // GROUP, one_group, 0)


def fetch(pieces, order_ref, source, sems, first=0):
    rows, columns = pieces[0].shape[0], source.shape[1]
    copies = []
    for i, piece in enumerate(pieces):
        at = pl.multiple_of(order_ref[i] * rows, rows)
        taken = piece.at[:, pl.ds(first, columns)]
        copies.append(pltpu.make_async_copy(taken, source.at[pl.ds(at, rows), :], sems.at[i]))
    return copies


def forward_kernel(steps, n_pieces, count_ref, rows_ref, cols_ref, order_ref, dests_ref, *refs):
    pieces, refs = refs[:n_pieces], refs[n_pieces:]
    values_ref, *outs, source, total, sems = refs
    step = pl.program_id(0)
    size = values_ref.shape[1]

    @pl.when(step == 0)
    def _():
        copies = fetch(pieces, order_ref, source, sems)
        for copy in copies:
            copy.start()
        total[...] = jnp.zeros_like(total)
        for copy in copies:
            copy.wait()

    def multiply(slot, block):
        at = pl.multiple_of(cols_ref[0, slot] * size, size)
        return lax.dot_general(
            block,
            source[:, pl.ds(at, size)],
            (((1,), (1,)), ((), ())),
            preferred_element_type=F32,
        )

    def accumulate(slot, product):
        total[rows_ref[0, slot]] += product

    for_live_slots(step, count_ref, values_ref, multiply, accumulate)

    @pl.when(step == steps - 1)
    def _():
        place = 0
        for out in outs:
            unit = total.shape[0] // len(PLACES)
            for first in range(0, out.shape[0] // size, unit):
                at = dests_ref[place] * unit
                for q in range(unit):
                    out[(first + q) * size : (first + q + 1) * size, :] = total[at + q].astype(BF16)
                place += 1


def backward_kernel(half, steps, n_pieces, count_ref, rows_ref, cols_ref, order_ref, *refs):
    pieces, refs = refs[:n_pieces], refs[n_pieces:]
    values_ref, *outs, source, total, sems = refs
    step = pl.program_id(0)
    size = values_ref.shape[1]

    @pl.when(step == 0)
    def _():
        copies = fetch(pieces, order_ref, source, sems, half * source.shape[1])
        for copy in copies:
            copy.start()
        total[...] = jnp.zeros_like(total)
        for copy in copies:
            copy.wait()

    def multiply(slot, block):
        at = pl.multiple_of(rows_ref[0, slot] * size, size)
        return lax.dot_general(
            source[pl.ds(at, size), :],
            block,
            (((0,), (0,)), ((), ())),
            preferred_element_type=F32,
        )

    def accumulate(slot, product):
        total[cols_ref[0, slot]] += product

    for_live_slots(step, count_ref, values_ref, multiply, accumulate)

    @pl.when(step == steps - 1)
    def _():
        def write(at, carry):
            columns = pl.ds(pl.multiple_of(at * size, size), size)
            first = 0
            for out in outs:
                out[:, columns] = total[at, first : first + out.shape[0], :].astype(BF16)
                first += out.shape[0]
            return carry

        lax.fori_loop(0, total.shape[0], write, 0)


def block_products(kernel, source_shape, total_shape, out_shapes, scalars, pieces, values):
    slots, size, _ = values.shape
    steps = slots // CHUNK

    def values_at(step, count_ref, *_):
        last = jnp.maximum((count_ref[0, 0] + CHUNK - 1) // CHUNK - 1, 0)
        return (jnp.minimum(step, last), 0, 0)

    return pl.pallas_call(
        functools.partial(kernel, steps, len(pieces)),
        out_shape=[jax.ShapeDtypeStruct(shape, BF16) for shape in out_shapes],
        grid_spec=pltpu.PrefetchScalarGridSpec(
            num_scalar_prefetch=len(scalars),
            grid=(steps,),
            in_specs=[pl.BlockSpec(memory_space=pl.ANY)] * len(pieces)
            + [pl.BlockSpec((CHUNK, size, size), values_at)],
            out_specs=[pl.BlockSpec(memory_space=pltpu.VMEM)] * len(out_shapes),
            scratch_shapes=[
                pltpu.VMEM(source_shape, BF16),
                pltpu.VMEM(total_shape, F32),
                pltpu.SemaphoreType.DMA((len(pieces),)),
            ],
        ),
        compiler_params=pltpu.CompilerParams(vmem_limit_bytes=52 * 1024 * 1024),
        cost_estimate=pl.CostEstimate(
            flops=4 * slots * size * size * 256,
            bytes_accessed=2 * slots * size * size,
            transcendentals=0,
        ),
    )(*scalars, *pieces, values)


def body(
    features, weight, bias, block_values, block_rows, block_cols, block_count, degrees, cotangent
):
    row, col = Axis("row", 2), Axis("col", 1)
    row_index, col_index = lax.axis_index("row"), lax.axis_index("col")
    values = block_values[0, 0]
    size = values.shape[1]
    rows_dev, width = cotangent.shape
    own = features.shape[1]
    panel_rows = rows_dev * col.size
    panel_cols = rows_dev * row.size
    nodes = rows_dev * row.size * col.size
    slots = (block_count, block_rows[0], block_cols[0])

    def scale_of(first, length):
        return 1.0 / jnp.sqrt(lax.dynamic_slice_in_dim(degrees, first, length, 0).astype(F32))

    scale_cols = scale_of(col_index * panel_cols, panel_cols)
    scale_own = scale_of(row_index * panel_rows + col_index * rows_dev, rows_dev)

    def picker(owners):
        picked = (jnp.stack(owners)[:, None] * own + jnp.arange(own)[None, :]).reshape(-1)
        return (picked[:, None] == jnp.arange(width)[None, :]).astype(BF16)

    scaled = (scale_cols[None, :] * features.T.astype(F32)).astype(BF16)
    dests = jnp.stack([col.index(r, p) for r, p in PLACES])

    def half_products(pieces):
        pieces = pieces + [row.swap(piece) for piece in pieces]
        return block_products(
            forward_kernel,
            (width // 2, panel_cols),
            (panel_rows // size, size, width // 2),
            [(2 * rows_dev, width // 2)] * 2 + [(rows_dev, width // 2)] * 4,
            slots + (jnp.arange(len(pieces), dtype=jnp.int32), dests),
            pieces,
            values,
        )

    near_pieces = gather_first(row, scaled)
    far_pieces = gather_second(row, near_pieces)
    partial = half_products(near_pieces)
    partial, far_pieces = lax.optimization_barrier((partial, far_pieces))
    arrived = scatter_first(col, *partial[:2])
    far_partial = half_products(far_pieces)
    far_partial, arrived = lax.optimization_barrier((far_partial, arrived))
    far_arrived = scatter_first(col, *far_partial[:2])
    reduced = scatter_second(col, *arrived, *[[part] for part in partial[2:]])
    far_reduced = scatter_second(col, *far_arrived, *[[part] for part in far_partial[2:]])
    reduced = jnp.concatenate([reduced, far_reduced], axis=1)
    aggregated = (scale_own[:, None] * reduced).astype(BF16)

    to_held = picker(
        [row.index(r, p, c) for half in (ORIGINS[:4], ORIGINS[4:]) for c in (0, 1) for r, p in half]
    )
    weight_held = jnp.dot(to_held, weight, preferred_element_type=F32).astype(BF16)
    pre = jnp.dot(aggregated, weight_held, preferred_element_type=F32) + bias
    sigma = jax.nn.sigmoid(pre)
    activations = (pre * sigma).astype(BF16)
    pre_grad = (cotangent.astype(F32) * sigma * (1.0 + pre * (1.0 - sigma))).astype(BF16)

    leave = (PLACES[:4], PLACES[4:])
    to_places = picker(
        [row.index(r, p, c) for places in leave for c in (1, 0) for r, p in places]
    )
    weight_places = jnp.dot(to_places, weight, preferred_element_type=F32).astype(BF16)
    scaled_grad = (
        scale_own[:, None] * jnp.dot(pre_grad, weight_places.T, preferred_element_type=F32)
    ).astype(BF16)
    pieces = gather_first(col, scaled_grad)
    pieces = pieces + gather_second(col, pieces)

    near = [(r, p - row.pair_at, c) for c in (0, 1) for r in range(RING) for p in (0, 1)]
    to_near = picker([row.index(*place) for place in near])
    to_near = jnp.dot(to_near, to_held.T, preferred_element_type=F32).astype(BF16)
    agg_near = lax.dot_general(
        aggregated, to_near, (((1,), (1,)), ((), ())), preferred_element_type=F32
    ).astype(BF16)
    terms = lax.dot_general(
        agg_near, pre_grad, (((0,), (0,)), ((), ())), preferred_element_type=F32
    )
    terms = terms[: width // 2] + row.swap(terms[width // 2 :])
    part = terms.shape[0] // RING
    terms = sum(
        [row.ring(terms[by * part : (by + 1) * part], by) for by in range(1, RING)], terms[:part]
    )
    pieces, terms = lax.optimization_barrier((pieces, terms))
    pairs = [terms, row.pair(terms), col.pair(terms), both_pairs(row, col, terms)]

    order = jnp.stack([col.index(r, p) for r, p in ORIGINS])
    def half_back(half, pieces, out_units):
        return block_products(
            functools.partial(backward_kernel, half),
            (panel_rows, width // 2),
            (panel_cols // size, width // 2, size),
            [(units * own, panel_cols) for units in out_units],
            slots + (order,),
            pieces,
            values,
        )

    from_here, sides, opposite = half_back(0, pieces, (4, 2, 2))
    from_here, pairs = lax.optimization_barrier((from_here, pairs))
    from_core = row.swap(from_here)
    terms = (pairs[0] + pairs[1]) + (pairs[2] + pairs[3])
    terms = (terms + col.ring(terms, 2)) + (col.ring(terms, 1) + col.ring(terms, 3))
    terms = terms * (1.0 / math.sqrt(nodes))
    from_core, terms = lax.optimization_barrier((from_core, terms))
    sides = add(sides, from_core[: 2 * own]).astype(BF16)
    opposite = add(opposite, from_core[2 * own :]).astype(BF16)
    sides, opposite, terms, pieces = lax.optimization_barrier((sides, opposite, terms, pieces))
    around = [terms] + [row.ring(terms, by) for by in range(1, RING)]
    arrived = scatter_first(row, sides, opposite)
    rest = half_back(1, pieces, (1,) * 8)
    rest, around = lax.optimization_barrier((rest, around))
    from_core = [row.swap(part) for part in rest[:3]]
    arrived, from_core = lax.optimization_barrier((arrived, from_core))
    from_core = from_core + [row.swap(rest[3])]
    reduced = scatter_second(row, *arrived, *[list(terms) for terms in zip(rest[4:], from_core)])
    feature_grad = (scale_cols[None, :] * reduced).astype(BF16).T
    terms = jnp.concatenate(around, axis=0)
    terms = jnp.concatenate([terms, row.swap(terms)], axis=0)
    held = jnp.zeros((row.size,), jnp.int32)
    for c in (0, 1):
        for by in range(RING):
            for p in (0, 1):
                owner = row.index(-by, p - row.pair_at, c)
                held = jnp.where(jnp.arange(row.size) == owner, (c * RING + by) * 2 + p, held)
    weight_grad = jnp.take(terms.reshape(row.size, own, width), held, axis=0).reshape(width, width)
    return (activations, weight_grad, feature_grad)


def solution(mesh):
    placed = (
        P("col", "row"),
        P(),
        P(),
        P("row", "col", None, None, None),
        P("row", "col", None),
        P("row", "col", None),
        P("row", "col"),
        P(),
        P(("row", "col"), None),
    )
    return jax.shard_map(
        body,
        mesh=mesh,
        in_specs=placed,
        out_specs=(P(("row", "col"), None), P(), P("col", "row")),
        check_vma=False,
    )
```

```python
import functools
import math

import jax
import jax.numpy as jnp
from jax import lax
from jax.experimental import pallas as pl
from jax.experimental.pallas import tpu as pltpu
from jax.sharding import PartitionSpec as P

BF16 = jnp.bfloat16
F32 = jnp.float32
CHUNK = 64
GROUP = 64
RING = 4
PLACES = ((1, 1), (3, 1), (2, 0), (2, 1), (1, 0), (3, 0), (0, 1), (0, 0))
ORIGINS = ((0, 0), (0, 1), (3, 0), (1, 0), (2, 0), (2, 1), (3, 1), (1, 1))


class Axis:
    def __init__(self, name, cores):
        self.name, self.cores = name, cores
        self.size = lax.axis_size(name)
        index = lax.axis_index(name)
        self.core = index % cores
        self.pair_at = index // cores % 2
        self.ring_at = index // (2 * cores)

    def index(self, ring, pair, core=0):
        at = (self.ring_at + ring) % RING * 2 + (self.pair_at + pair) % 2
        return at * self.cores + (self.core + core) % self.cores

    def ring(self, x, by):
        step = 2 * self.cores
        return lax.ppermute(x, self.name, [(i, (i + by * step) % self.size) for i in range(self.size)])

    def pair(self, x):
        return lax.ppermute(x, self.name, [(i, i ^ self.cores) for i in range(self.size)])

    def swap(self, x):
        return lax.ppermute(x, self.name, [(i, i ^ 1) for i in range(self.size)])


def both_pairs(row, col, x):
    n = col.size
    to = [
        (r * n + c, (r ^ row.cores) * n + (c ^ col.cores))
        for r in range(row.size)
        for c in range(n)
    ]
    return lax.ppermute(x, (row.name, col.name), to)


def add(*terms):
    return functools.reduce(jnp.add, [term.astype(F32) for term in terms])


def gather_first(axis, x):
    return list(
        lax.optimization_barrier((x, axis.pair(x), axis.ring(x, 1), axis.ring(x, 3)))
    )


def gather_second(axis, first):
    x, across, one, three = first
    return [axis.ring(x, 2), axis.ring(across, 2), axis.pair(one), axis.pair(three)]


def scatter_first(axis, sides, opposite):
    return axis.pair(sides), axis.ring(opposite, 2)


def scatter_second(axis, sides, opposite, one, three, across, own):
    n = own[0].shape[0]
    one = axis.ring(add(*one, sides[:n]).astype(BF16), 1)
    three = axis.ring(add(*three, sides[n:]).astype(BF16), 3)
    across = axis.pair(add(*across, opposite[n:]).astype(BF16))
    return add(*own, opposite[:n], one, three, across)


def for_live_slots(step, count_ref, values_ref, multiply, accumulate):
    base = step * CHUNK
    count = count_ref[0, 0]
    here = jnp.clip(count - base, 0, CHUNK)

    def one_group(turn, carry):
        first = turn * GROUP
        products = []
        for u in range(GROUP):
            block = values_ref[first + u]
            block = jnp.where(base + first + u < count, block, jnp.zeros_like(block))
            products.append(multiply(base + first + u, block))
        for u in range(GROUP):
            accumulate(base + first + u, products[u])
        return carry

    lax.fori_loop(0, (here + GROUP - 1) // GROUP, one_group, 0)


def fetch(pieces, order_ref, source, sems, first=0):
    rows, columns = pieces[0].shape[0], source.shape[1]
    copies = []
    for i, piece in enumerate(pieces):
        at = pl.multiple_of(order_ref[i] * rows, rows)
        taken = piece.at[:, pl.ds(first, columns)]
        copies.append(pltpu.make_async_copy(taken, source.at[pl.ds(at, rows), :], sems.at[i]))
    return copies


def forward_kernel(steps, n_pieces, count_ref, rows_ref, cols_ref, order_ref, dests_ref, *refs):
    pieces, refs = refs[:n_pieces], refs[n_pieces:]
    values_ref, *outs, source, total, sems = refs
    step = pl.program_id(0)
    size = values_ref.shape[1]

    @pl.when(step == 0)
    def _():
        copies = fetch(pieces, order_ref, source, sems)
        for copy in copies:
            copy.start()
        total[...] = jnp.zeros_like(total)
        for copy in copies:
            copy.wait()

    def multiply(slot, block):
        at = pl.multiple_of(cols_ref[0, slot] * size, size)
        return lax.dot_general(
            block,
            source[:, pl.ds(at, size)],
            (((1,), (1,)), ((), ())),
            preferred_element_type=F32,
        )

    def accumulate(slot, product):
        total[rows_ref[0, slot]] += product

    for_live_slots(step, count_ref, values_ref, multiply, accumulate)

    @pl.when(step == steps - 1)
    def _():
        place = 0
        for out in outs:
            unit = total.shape[0] // len(PLACES)
            for first in range(0, out.shape[0] // size, unit):
                at = dests_ref[place] * unit
                for q in range(unit):
                    out[(first + q) * size : (first + q + 1) * size, :] = total[at + q].astype(BF16)
                place += 1


def backward_kernel(half, steps, n_pieces, count_ref, rows_ref, cols_ref, order_ref, *refs):
    pieces, refs = refs[:n_pieces], refs[n_pieces:]
    values_ref, *outs, source, total, sems = refs
    step = pl.program_id(0)
    size = values_ref.shape[1]

    @pl.when(step == 0)
    def _():
        copies = fetch(pieces, order_ref, source, sems, half * source.shape[1])
        for copy in copies:
            copy.start()
        total[...] = jnp.zeros_like(total)
        for copy in copies:
            copy.wait()

    def multiply(slot, block):
        at = pl.multiple_of(rows_ref[0, slot] * size, size)
        return lax.dot_general(
            source[pl.ds(at, size), :],
            block,
            (((0,), (0,)), ((), ())),
            preferred_element_type=F32,
        )

    def accumulate(slot, product):
        total[cols_ref[0, slot]] += product

    for_live_slots(step, count_ref, values_ref, multiply, accumulate)

    @pl.when(step == steps - 1)
    def _():
        def write(at, carry):
            columns = pl.ds(pl.multiple_of(at * size, size), size)
            first = 0
            for out in outs:
                out[:, columns] = total[at, first : first + out.shape[0], :].astype(BF16)
                first += out.shape[0]
            return carry

        lax.fori_loop(0, total.shape[0], write, 0)


def block_products(kernel, source_shape, total_shape, out_shapes, scalars, pieces, values):
    slots, size, _ = values.shape
    steps = slots // CHUNK

    def values_at(step, count_ref, *_):
        last = jnp.maximum((count_ref[0, 0] + CHUNK - 1) // CHUNK - 1, 0)
        return (jnp.minimum(step, last), 0, 0)

    return pl.pallas_call(
        functools.partial(kernel, steps, len(pieces)),
        out_shape=[jax.ShapeDtypeStruct(shape, BF16) for shape in out_shapes],
        grid_spec=pltpu.PrefetchScalarGridSpec(
            num_scalar_prefetch=len(scalars),
            grid=(steps,),
            in_specs=[pl.BlockSpec(memory_space=pl.ANY)] * len(pieces)
            + [pl.BlockSpec((CHUNK, size, size), values_at)],
            out_specs=[pl.BlockSpec(memory_space=pltpu.VMEM)] * len(out_shapes),
            scratch_shapes=[
                pltpu.VMEM(source_shape, BF16),
                pltpu.VMEM(total_shape, F32),
                pltpu.SemaphoreType.DMA((len(pieces),)),
            ],
        ),
        compiler_params=pltpu.CompilerParams(vmem_limit_bytes=52 * 1024 * 1024),
        cost_estimate=pl.CostEstimate(
            flops=4 * slots * size * size * 256,
            bytes_accessed=2 * slots * size * size,
            transcendentals=0,
        ),
    )(*scalars, *pieces, values)


def body(
    features, weight, bias, block_values, block_rows, block_cols, block_count, degrees, cotangent
):
    row, col = Axis("row", 2), Axis("col", 1)
    row_index, col_index = lax.axis_index("row"), lax.axis_index("col")
    values = block_values[0, 0]
    size = values.shape[1]
    rows_dev, width = cotangent.shape
    own = features.shape[1]
    panel_rows = rows_dev * col.size
    panel_cols = rows_dev * row.size
    nodes = rows_dev * row.size * col.size
    slots = (block_count, block_rows[0], block_cols[0])

    def scale_of(first, length):
        return 1.0 / jnp.sqrt(lax.dynamic_slice_in_dim(degrees, first, length, 0).astype(F32))

    scale_cols = scale_of(col_index * panel_cols, panel_cols)
    scale_own = scale_of(row_index * panel_rows + col_index * rows_dev, rows_dev)

    def picker(owners):
        picked = (jnp.stack(owners)[:, None] * own + jnp.arange(own)[None, :]).reshape(-1)
        return (picked[:, None] == jnp.arange(width)[None, :]).astype(BF16)

    scaled = (scale_cols[None, :] * features.T.astype(F32)).astype(BF16)
    dests = jnp.stack([col.index(r, p) for r, p in PLACES])

    def half_products(pieces):
        pieces = pieces + [row.swap(piece) for piece in pieces]
        return block_products(
            forward_kernel,
            (width // 2, panel_cols),
            (panel_rows // size, size, width // 2),
            [(2 * rows_dev, width // 2)] * 2 + [(rows_dev, width // 2)] * 4,
            slots + (jnp.arange(len(pieces), dtype=jnp.int32), dests),
            pieces,
            values,
        )

    near_pieces = gather_first(row, scaled)
    far_pieces = gather_second(row, near_pieces)
    partial = half_products(near_pieces)
    partial, far_pieces = lax.optimization_barrier((partial, far_pieces))
    arrived = scatter_first(col, *partial[:2])
    far_partial = half_products(far_pieces)
    far_partial, arrived = lax.optimization_barrier((far_partial, arrived))
    far_arrived = scatter_first(col, *far_partial[:2])
    reduced = scatter_second(col, *arrived, *[[part] for part in partial[2:]])
    far_reduced = scatter_second(col, *far_arrived, *[[part] for part in far_partial[2:]])
    reduced = jnp.concatenate([reduced, far_reduced], axis=1)
    aggregated = (scale_own[:, None] * reduced).astype(BF16)

    to_held = picker(
        [row.index(r, p, c) for half in (ORIGINS[:4], ORIGINS[4:]) for c in (0, 1) for r, p in half]
    )
    weight_held = jnp.dot(to_held, weight, preferred_element_type=F32).astype(BF16)
    pre = jnp.dot(aggregated, weight_held, preferred_element_type=F32) + bias
    sigma = jax.nn.sigmoid(pre)
    activations = (pre * sigma).astype(BF16)
    pre_grad = (cotangent.astype(F32) * sigma * (1.0 + pre * (1.0 - sigma))).astype(BF16)

    leave = (PLACES[:4], PLACES[4:])
    to_places = picker(
        [row.index(r, p, c) for places in leave for c in (1, 0) for r, p in places]
    )
    weight_places = jnp.dot(to_places, weight, preferred_element_type=F32).astype(BF16)
    scaled_grad = (
        scale_own[:, None] * jnp.dot(pre_grad, weight_places.T, preferred_element_type=F32)
    ).astype(BF16)
    pieces = gather_first(col, scaled_grad)
    pieces = pieces + gather_second(col, pieces)

    near = [(r, p - row.pair_at, c) for c in (0, 1) for r in range(RING) for p in (0, 1)]
    to_near = picker([row.index(*place) for place in near])
    to_near = jnp.dot(to_near, to_held.T, preferred_element_type=F32).astype(BF16)
    agg_near = lax.dot_general(
        aggregated, to_near, (((1,), (1,)), ((), ())), preferred_element_type=F32
    ).astype(BF16)
    terms = lax.dot_general(
        agg_near, pre_grad, (((0,), (0,)), ((), ())), preferred_element_type=F32
    )
    terms = terms[: width // 2] + row.swap(terms[width // 2 :])
    part = terms.shape[0] // RING
    terms = sum(
        [row.ring(terms[by * part : (by + 1) * part], by) for by in range(1, RING)], terms[:part]
    )
    pieces, terms = lax.optimization_barrier((pieces, terms))
    pairs = [terms, row.pair(terms), col.pair(terms), both_pairs(row, col, terms)]

    order = jnp.stack([col.index(r, p) for r, p in ORIGINS])
    def half_back(half, pieces, out_units):
        return block_products(
            functools.partial(backward_kernel, half),
            (panel_rows, width // 2),
            (panel_cols // size, width // 2, size),
            [(units * own, panel_cols) for units in out_units],
            slots + (order,),
            pieces,
            values,
        )

    from_here, sides, opposite = half_back(0, pieces, (4, 2, 2))
    from_here, pairs = lax.optimization_barrier((from_here, pairs))
    from_core = row.swap(from_here)
    terms = (pairs[0] + pairs[1]) + (pairs[2] + pairs[3])
    terms = (terms + col.ring(terms, 2)) + (col.ring(terms, 1) + col.ring(terms, 3))
    terms = terms * (1.0 / math.sqrt(nodes))
    from_core, terms = lax.optimization_barrier((from_core, terms))
    sides = add(sides, from_core[: 2 * own]).astype(BF16)
    opposite = add(opposite, from_core[2 * own :]).astype(BF16)
    sides, opposite, terms, pieces = lax.optimization_barrier((sides, opposite, terms, pieces))
    arrived = scatter_first(row, sides, opposite)
    rest = half_back(1, pieces, (1,) * 8)
    rest, terms = lax.optimization_barrier((rest, terms))
    around = [terms] + [row.ring(terms, by) for by in range(1, RING)]
    from_core = [row.swap(part) for part in rest[:3]]
    arrived, from_core = lax.optimization_barrier((arrived, from_core))
    from_core = from_core + [row.swap(rest[3])]
    reduced = scatter_second(row, *arrived, *[list(terms) for terms in zip(rest[4:], from_core)])
    feature_grad = (scale_cols[None, :] * reduced).astype(BF16).T
    terms = jnp.concatenate(around, axis=0)
    terms = jnp.concatenate([terms, row.swap(terms)], axis=0)
    held = jnp.zeros((row.size,), jnp.int32)
    for c in (0, 1):
        for by in range(RING):
            for p in (0, 1):
                owner = row.index(-by, p - row.pair_at, c)
                held = jnp.where(jnp.arange(row.size) == owner, (c * RING + by) * 2 + p, held)
    weight_grad = jnp.take(terms.reshape(row.size, own, width), held, axis=0).reshape(width, width)
    return (activations, weight_grad, feature_grad)


def solution(mesh):
    placed = (
        P("col", "row"),
        P(),
        P(),
        P("row", "col", None, None, None),
        P("row", "col", None),
        P("row", "col", None),
        P("row", "col"),
        P(),
        P(("row", "col"), None),
    )
    return jax.shard_map(
        body,
        mesh=mesh,
        in_specs=placed,
        out_specs=(P(("row", "col"), None), P(), P("col", "row")),
        check_vma=False,
    )
```
